256 devices in a mesh: row: 32 (over y_hi, z, core), col: 8 (over y_lo, x).
Axes of the slice: x: 4, y: 4 (y_hi: 2, y_lo: 2; y = y_hi * 2 + y_lo), z: 8, core: 2. Of those that a mesh axis runs over, the one named last changes fastest.
Arguments:
- left_panel: float32 [8192, 512], P('row', 'col'), may hold values from -0.25 to 0.25
- accum: float32 [8192, 8192], P('row', 'col'), may hold values from -6 to 6
- col_scale: float32 [8192], P('col'), may hold values from 0.3 to 3
Outputs:
- scaled_square: float32 [8192, 8192], P('row', 'col')
The draws below stay inside these ranges and needn't reach their ends.
All inputs are finite; a program needn't handle non-finite values.
Results may differ from the reference program's by a relative error of at most 0.00005.
Values sent between devices are 32-bit elements; how exact they have to be, the bound alone decides.
No kernel may reach another device: no remote copies, remote signals or barrier semaphores. Data moves between devices by JAX's collectives and lax.ppermute only.
A program may use at most 64 MiB of HBM per device.

```python
import math
import jax
import jax.numpy as jnp
from jax import lax

PANEL = 256
ROWS = 8192


def steps_of(key, shape, split, smallest, high):
    level, own = 1.0, jax.random.fold_in(key, 6)
    for dim, parts in split:
        heights = jnp.exp(jax.random.uniform(jax.random.fold_in(own, dim), (parts,), jnp.float32, smallest / len(split), high / len(split)))
        level = level * jnp.repeat(heights, shape[dim] // parts).reshape([-1 if axis == dim else 1 for axis in range(len(shape))])
    return level


def bell_draw(rng, dims, deviation, reach, split=(), held_as=jnp.bfloat16):
    factor_of = steps_of(rng, dims, split, -0.22, 0.18) if split else 1.0
    drawn = jax.random.normal(rng, dims, jnp.float32) * deviation * factor_of
    return jnp.minimum(jnp.maximum(drawn, -reach), reach).astype(held_as)


def setup_inputs(seed: int = 0) -> dict:
    streams_of = jax.random.split(jax.random.key(seed), 4)
    return {
        "left_panel": bell_draw(streams_of[0], (ROWS, 2 * PANEL), (2 * PANEL) ** -0.5, 0.25, ((0, 32), (1, 8)), jnp.float32),
        "accum": bell_draw(streams_of[1], (ROWS, ROWS), 1.0, 6.0, ((0, 32), (1, 8)), jnp.float32),
        "col_scale": jnp.clip(jnp.exp(math.log(3.0) - 2.3025851 * jax.random.uniform(streams_of[2], (ROWS,), jnp.float32) ** steps_of(streams_of[2], (ROWS,), ((0, 8),), -0.2, 0.2)), 0.3, 3.0),
    }


def reference(left_panel, accum, col_scale):
    square = lax.dot_general(left_panel, left_panel, (((1,), (1,)), ((), ())), precision=lax.Precision.HIGHEST, preferred_element_type=jnp.float32)
    mixed = accum + square
    scaled = mixed * col_scale[None, :]
    norms = lax.optimization_barrier(jnp.mean(scaled * scaled, axis=1))
    return scaled * lax.rsqrt(norms + 1e-06)[:, None]
```

```python
import jax
import jax.numpy as jnp
from jax import lax
from jax.experimental import pallas as pl
from jax.experimental.pallas import tpu as pltpu
from jax.sharding import Mesh, PartitionSpec as P

YH, Z, CORE, YL, X = 2, 8, 2, 2, 4
ROW = ("yh", "z", "core")
COL = ("yl", "x")
VMEM = pl.BlockSpec(memory_space=pltpu.VMEM)
SMEM = pl.BlockSpec(memory_space=pltpu.SMEM)


def along_z(shift):
    pairs = []
    for yh in range(YH):
        for z in range(Z):
            for yl in range(YL):
                source = (yh * Z + z) * YL + yl
                target = (yl * Z + (z + shift) % Z) * YL + yh
                pairs.append((source, target))
    return pairs


def sort_planes(z_ref, *refs):
    pieces, out_ref = refs[:-1], refs[-1]
    for shift, piece in enumerate(pieces):
        plane = lax.rem(z_ref[0] + Z - shift, Z)
        value = piece[...]
        for copy in range(YH):
            out_ref[copy, plane] = value


def split(value):
    high = value.astype(jnp.bfloat16)
    low = (value - high.astype(jnp.float32)).astype(jnp.bfloat16)
    return high, low


def times(a, b):
    return lax.dot_general(a, b, (((0,), (0,)), ((), ())), preferred_element_type=jnp.float32)


def product(core_ref, rows_ref, own_ref, other_ref, accum_ref, scale_ref, scaled_ref, sums_ref):
    depth = rows_ref.shape[0] * rows_ref.shape[1]
    rows, width = rows_ref.shape[2], own_ref.shape[3]
    high, low = split(rows_ref[...].reshape(depth, rows))
    squares = jnp.zeros((rows, 128), jnp.float32)
    for half in range(2):
        for which in range(CORE):
            mine = core_ref[0] == which
            block = jnp.where(mine, own_ref[:, half], other_ref[:, half]).reshape(depth, width)
            block_high, block_low = split(block)
            part = times(high, block_high) + (times(high, block_low) + times(low, block_high))
            cols = pl.ds((half * CORE + which) * width, width)
            scaled = (accum_ref[:, cols] + part) * scale_ref[:, cols]
            scaled_ref[:, cols] = scaled
            for lane in range(0, width, 128):
                chunk = scaled[:, lane : lane + 128]
                squares += chunk * chunk
    sums = jnp.sum(squares.T, axis=0, keepdims=True)
    sums_ref[...] = jnp.broadcast_to(sums[None], sums_ref.shape)


def divide(scaled_ref, sums_ref, out_ref):
    rows, cols = scaled_ref.shape
    total = jnp.sum(sums_ref[...], axis=0)[:1]
    count = cols * sums_ref.shape[0]
    factor = lax.rsqrt(total / count + 1e-06)
    factor = jnp.broadcast_to(factor, (128, rows)).T
    for lane in range(0, cols, 128):
        out_ref[:, lane : lane + 128] = scaled_ref[:, lane : lane + 128] * factor


def call(kernel, out_shape, inputs, flops=0, scalars=1):
    return pl.pallas_call(
        kernel,
        out_shape=out_shape,
        in_specs=[SMEM] * scalars + [VMEM] * (len(inputs) - scalars),
        out_specs=jax.tree.map(lambda _: VMEM, out_shape),
        compiler_params=pltpu.CompilerParams(vmem_limit_bytes=32 * 1024 * 1024),
        cost_estimate=pl.CostEstimate(flops=flops, bytes_accessed=2 * 1024 * 1024, transcendentals=0),
    )(*inputs)


def f32(*shape):
    return jax.ShapeDtypeStruct(shape, jnp.float32)


def per_device(left_panel, accum, col_scale):
    block = left_panel.T
    depth, rows = block.shape
    cols = accum.shape[1]
    groups = YL * X
    pieces = [lax.ppermute(block, ("yh", "z", "yl"), along_z(shift)) for shift in range(Z)]
    copies = jnp.broadcast_to(block[None], (groups, depth, rows))
    full_rows = lax.all_to_all(copies, COL, 0, 0)

    z = lax.axis_index("z").reshape(1)
    core = lax.axis_index("core").reshape(1)
    planes = call(sort_planes, f32(YH, Z, depth, rows), [z, *pieces])
    planes = planes.reshape(YH * X, Z // X, depth, rows)
    own = lax.all_to_all(planes, ("yh", "x"), 0, 0)
    other = lax.ppermute(own, "core", [(0, 1), (1, 0)])

    scaled, sums = call(
        product,
        (f32(rows, cols), f32(groups, 8, rows)),
        [core, full_rows, own, other, accum, col_scale[None]],
        flops=6 * rows * cols * depth * groups,
    )
    sums = lax.all_to_all(sums, COL, 0, 0)
    return call(divide, f32(rows, cols), [scaled, sums], scalars=0)


def solution(mesh):
    fine = Mesh(mesh.devices.reshape(YH, Z, CORE, YL, X), (*ROW, *COL))
    placed = (P(ROW, COL), P(ROW, COL), P(COL))
    return jax.shard_map(
        per_device, mesh=fine, in_specs=placed, out_specs=P(ROW, COL), check_vma=False
    )
```

```python
import itertools

import jax
import jax.numpy as jnp
from jax import lax
from jax.experimental import pallas as pl
from jax.experimental.pallas import tpu as pltpu
from jax.sharding import Mesh, PartitionSpec as P

YH, Z, CORE, YL, X = SIZES = 2, 8, 2, 2, 4
ROW = ("yh", "z", "core")
COL = ("yl", "x")
ALL = (*ROW, *COL)
NEAR = (1, 2, 3)
VMEM = pl.BlockSpec(memory_space=pltpu.VMEM)
SMEM = pl.BlockSpec(memory_space=pltpu.SMEM)


def send(value, target):
    def index(place):
        found = 0
        for at, size in zip(place, SIZES, strict=True):
            found = found * size + at
        return found

    pairs = [(index(place), index(target(*place))) for place in itertools.product(*map(range, SIZES))]
    return lax.ppermute(value, ALL, pairs)


def across(yh, z, core, yl, x):
    return yh, z, 1 - core, yl, x


def turned(yh, z, core, yl, x):
    return yl, z, core, yh, x


def opposite(yh, z, core, yl, x):
    return yl, (z + Z // 2) % Z, core, yh, x


def along_z(hops):
    def target(yh, z, core, yl, x):
        return yl, (z + (hops if core == 0 else -hops)) % Z, core, yh, x

    return target


def in_plane(step):
    def target(yh, z, core, yl, x):
        return yh ^ core ^ (step // 2), z, core, yl, (x + step) % X

    return target


def sort_planes(place_ref, here_ref, here_beside_ref, far_ref, far_beside_ref, *refs):
    near, near_beside = refs[: len(NEAR)], refs[len(NEAR) : 2 * len(NEAR)]
    outs, sorted_ref = refs[2 * len(NEAR) : -1], refs[-1]
    z, core, x = (place_ref[i] for i in range(3))

    def put(plane, row_core, value):
        plane = lax.rem(plane + 2 * Z, Z)
        sorted_ref[lax.rem(plane // 2 - x + X, X), lax.rem(plane, 2), row_core] = value

    put(z, core, here_ref[...])
    put(z, 1 - core, here_beside_ref[...])
    put(z + Z // 2, core, far_ref[...])
    put(z + Z // 2, 1 - core, far_beside_ref[...])
    for hops, piece, piece_beside in zip(NEAR, near, near_beside, strict=True):
        plane = z + (2 * core - 1) * hops
        plane_beside = z - (2 * core - 1) * hops
        put(plane, core, piece[0])
        put(plane, 1 - core, piece[1])
        put(plane_beside, 1 - core, piece_beside[0])
        put(plane_beside, core, piece_beside[1])
    for step, out in enumerate(outs):
        out[...] = sorted_ref[step]


def split(value):
    high = value.astype(jnp.bfloat16)
    low = (value - high.astype(jnp.float32)).astype(jnp.bfloat16)
    return high, low


def times(a, b):
    return lax.dot_general(a, b, (((0,), (0,)), ((), ())), preferred_element_type=jnp.float32)


def product(place_ref, rows_ref, accum_ref, scale_ref, *refs):
    pieces, (scaled_ref, sums_ref) = refs[: 2 * X], refs[2 * X :]
    yh, core, x = (place_ref[i] for i in range(3))
    ordered = []
    for flip in (core, 1 - core):
        for step in range(X):
            ordered.append(rows_ref[lax.rem(yh + flip + step // 2, 2) * X + lax.rem(x - step + X, X)])
    high, low = split(jnp.concatenate(ordered, axis=0))
    rows, width = rows_ref.shape[2], pieces[0].shape[3]
    squares = jnp.zeros((rows, 128), jnp.float32)
    for odd in range(2):
        for row_core in range(CORE):
            block = jnp.concatenate([piece[odd, row_core] for piece in pieces], axis=0)
            block_high, block_low = split(block)
            part = times(high, block_high) + (times(high, block_low) + times(low, block_high))
            cols = pl.ds((odd * CORE + row_core) * width, width)
            scaled = (accum_ref[:, cols] + part) * scale_ref[:, cols]
            scaled_ref[:, cols] = scaled
            for lane in range(0, width, 128):
                chunk = scaled[:, lane : lane + 128]
                squares += chunk * chunk
    sums = jnp.sum(squares.T, axis=0, keepdims=True)
    sums_ref[...] = jnp.broadcast_to(sums[None], sums_ref.shape)


def divide(scaled_ref, sums_ref, out_ref):
    rows, cols = scaled_ref.shape
    total = jnp.sum(sums_ref[...], axis=0)[:1]
    count = cols * sums_ref.shape[0]
    factor = lax.rsqrt(total / count + 1e-06)
    factor = jnp.broadcast_to(factor, (128, rows)).T
    for lane in range(0, cols, 128):
        out_ref[:, lane : lane + 128] = scaled_ref[:, lane : lane + 128] * factor


def call(kernel, out_shape, inputs, scalars=1, scratch=(), flops=0):
    return pl.pallas_call(
        kernel,
        out_shape=out_shape,
        in_specs=[SMEM] * scalars + [VMEM] * (len(inputs) - scalars),
        out_specs=jax.tree.map(lambda _: VMEM, out_shape),
        scratch_shapes=list(scratch),
        compiler_params=pltpu.CompilerParams(vmem_limit_bytes=16 * 1024 * 1024),
        cost_estimate=pl.CostEstimate(flops=flops, bytes_accessed=2 * 1024 * 1024, transcendentals=0),
    )(*inputs)


def f32(*shape):
    return jax.ShapeDtypeStruct(shape, jnp.float32)


def place(*names):
    return jnp.stack([lax.axis_index(name) for name in names])


def per_device(left_panel, accum, col_scale):
    block = left_panel.T
    depth, rows = block.shape
    cols = accum.shape[1]
    groups = YL * X

    copies = jnp.broadcast_to(block[None], (groups, depth, rows))
    full_rows = lax.all_to_all(copies, COL, 0, 0)
    here = send(block, turned)
    both = jnp.stack([block, send(block, across)])
    near = [send(both, along_z(hops)) for hops in NEAR]
    far = send(block, opposite)
    far_beside = send(far, across)
    here_beside = send(here, across)
    near_beside = [send(piece, across) for piece in near]

    planes = call(
        sort_planes,
        (f32(2, CORE, depth, rows),) * X,
        [place("z", "core", "x"), here, here_beside, far, far_beside, *near, *near_beside],
        scratch=[pltpu.VMEM((X, 2, CORE, depth, rows), jnp.float32)],
    )
    mine = [send(planes[step], in_plane(step)) for step in range(X)]
    others = [send(piece, across) for piece in mine]

    scaled, sums = call(
        product,
        (f32(rows, cols), f32(groups, 8, rows)),
        [place("yh", "core", "x"), full_rows, accum, col_scale[None], *mine, *others],
        flops=6 * rows * cols * depth * groups,
    )
    sums = lax.all_to_all(sums, COL, 0, 0)
    return call(divide, f32(rows, cols), [scaled, sums], scalars=0)


def solution(mesh):
    fine = Mesh(mesh.devices.reshape(SIZES), ALL)
    placed = (P(ROW, COL), P(ROW, COL), P(COL))
    return jax.shard_map(
        per_device, mesh=fine, in_specs=placed, out_specs=P(ROW, COL), check_vma=False
    )
```

```python
import itertools

import jax
import jax.numpy as jnp
from jax import lax
from jax.experimental import pallas as pl
from jax.experimental.pallas import tpu as pltpu
from jax.sharding import Mesh, PartitionSpec as P

YH, Z, CORE, YL, X = SIZES = 2, 8, 2, 2, 4
ROW = ("yh", "z", "core")
COL = ("yl", "x")
ALL = (*ROW, *COL)
VMEM = pl.BlockSpec(memory_space=pltpu.VMEM)
SMEM = pl.BlockSpec(memory_space=pltpu.SMEM)


def send(value, target):
    def index(place):
        found = 0
        for at, size in zip(place, SIZES, strict=True):
            found = found * size + at
        return found

    pairs = [(index(place), index(target(*place))) for place in itertools.product(*map(range, SIZES))]
    return lax.ppermute(value, ALL, pairs)


def across(yh, z, core, yl, x):
    return yh, z, 1 - core, yl, x


def turned(yh, z, core, yl, x):
    return yl, z, core, yh, x


def opposite(yh, z, core, yl, x):
    return yl, (z + Z // 2) % Z, core, yh, x


def along_z(hops):
    def target(yh, z, core, yl, x):
        return yl, (z + (hops if core == 0 else -hops)) % Z, core, yh, x

    return target


def pass_on(yh, z, core, yl, x):
    return yh, (z + (1 if core == 0 else -1)) % Z, core, yl, x


def along_x(hops):
    def target(yh, z, core, yl, x):
        return yh, z, core, yl, (x + (hops if core == 0 else -hops)) % X

    return target


def along_y(yh, z, core, yl, x):
    return 1 - yh, z, core, yl, x


def along_yl(yh, z, core, yl, x):
    return yh, z, core, 1 - yl, x


def sort_planes(place_ref, here_ref, here_beside_ref, far_ref, far_beside_ref, near_ref, near_beside_ref, stay_ref, next_ref, second_ref, sorted_ref):
    z, core, x = (place_ref[i] for i in range(3))
    turn = 2 * core - 1

    def put(pair_hops, row_core, value):
        sorted_ref[lax.rem(z // 2 + pair_hops - x + 2 * X, X), row_core] = value

    put(0, core, here_ref[...])
    put(0, 1 - core, here_beside_ref[...])
    put(X // 2, core, far_ref[...])
    put(X // 2, 1 - core, far_beside_ref[...])
    put(turn, core, near_ref[0])
    put(turn, 1 - core, near_ref[1])
    put(-turn, 1 - core, near_beside_ref[0])
    put(-turn, core, near_beside_ref[1])
    stay_ref[...] = sorted_ref[0, core]
    next_ref[...] = sorted_ref[1 + 2 * core]
    second_ref[...] = sorted_ref[X // 2, core]


def split(value):
    high = value.astype(jnp.bfloat16)
    low = (value - high.astype(jnp.float32)).astype(jnp.bfloat16)
    return high, low


def times(a, b):
    return lax.dot_general(a, b, (((0,), (0,)), ((), ())), preferred_element_type=jnp.float32)


def product(place_ref, rows_ref, rows_yl_ref, rows_beside_ref, rows_yl_beside_ref, accum_ref, scale_ref, *refs):
    mine, others, (scaled_ref, sums_ref) = refs[:4], refs[4:8], refs[8:]
    yh, z, core, yl = (place_ref[i] for i in range(4))
    def rows_of(own, beside):
        return [own[0], own[1], beside[2], own[3]]

    here, there = rows_of(rows_ref, rows_beside_ref), rows_of(rows_yl_ref, rows_yl_beside_ref)
    first = [jnp.where(yh == yl, a, b) for a, b in zip(here, there, strict=True)]
    second = [jnp.where(yh == yl, b, a) for a, b in zip(here, there, strict=True)]
    high, low = split(jnp.concatenate(first + second, axis=0))

    def blocks_of(pack, beside):
        one, two = mine[pack], others[pack]
        near, row_core = (one, two)[beside], lax.rem(core + beside, CORE)
        return [near[0], one[1 + row_core], two[1 + row_core], near[3]]

    rows, width = rows_ref.shape[2], refs[0].shape[2]
    squares = jnp.zeros((rows, 128), jnp.float32)
    for odd in range(2):
        for beside in range(CORE):
            block = jnp.concatenate(blocks_of(2 * odd, beside) + blocks_of(2 * odd + 1, beside), axis=0)
            block_high, block_low = split(block)
            part = times(high, block_high) + (times(high, block_low) + times(low, block_high))
            tile = lax.rem(z + odd, 2) * CORE + lax.rem(core + beside, CORE)
            cols = pl.ds(pl.multiple_of(tile * width, width), width)
            scaled = (accum_ref[:, cols] + part) * scale_ref[:, cols]
            scaled_ref[:, cols] = scaled
            for lane in range(0, width, 128):
                chunk = scaled[:, lane : lane + 128]
                squares += chunk * chunk
    sums = jnp.sum(squares.T, axis=0, keepdims=True)
    sums_ref[...] = jnp.broadcast_to(sums[None], sums_ref.shape)


def divide(scaled_ref, sums_ref, out_ref):
    rows, cols = scaled_ref.shape
    total = jnp.sum(sums_ref[...], axis=0)[:1]
    count = cols * sums_ref.shape[0]
    factor = lax.rsqrt(total / count + 1e-06)
    factor = jnp.broadcast_to(factor, (128, rows)).T
    for lane in range(0, cols, 128):
        out_ref[:, lane : lane + 128] = scaled_ref[:, lane : lane + 128] * factor


def call(kernel, out_shape, inputs, scalars=1, scratch=(), flops=0):
    return pl.pallas_call(
        kernel,
        out_shape=out_shape,
        in_specs=[SMEM] * scalars + [VMEM] * (len(inputs) - scalars),
        out_specs=jax.tree.map(lambda _: VMEM, out_shape),
        scratch_shapes=list(scratch),
        compiler_params=pltpu.CompilerParams(vmem_limit_bytes=16 * 1024 * 1024),
        cost_estimate=pl.CostEstimate(flops=flops, bytes_accessed=2 * 1024 * 1024, transcendentals=0),
    )(*inputs)


def f32(*shape):
    return jax.ShapeDtypeStruct(shape, jnp.float32)


def place(*names):
    return jnp.stack([lax.axis_index(name) for name in names])


def per_device(left_panel, accum, col_scale):
    block = left_panel.T
    depth, rows = block.shape
    cols = accum.shape[1]
    groups = YL * X

    here = send(block, turned)
    both = jnp.stack([block, send(block, across)])
    near = send(both, along_z(2))
    rows_next = send(both, along_x(1))
    rows_second = send(block, along_x(X // 2))
    far = send(block, opposite)
    here_beside, far_beside, near_beside = (send(piece, across) for piece in (here, far, near))

    stay, to_next, to_second = call(
        sort_planes,
        (f32(depth, rows), f32(CORE, depth, rows), f32(depth, rows)),
        [place("z", "core", "x"), here, here_beside, far, far_beside, near, near_beside],
        scratch=[pltpu.VMEM((X, CORE, depth, rows), jnp.float32)],
    )
    from_next = send(to_next, along_x(1))
    from_second = send(to_second, along_x(X // 2))
    kept = jnp.concatenate([stay[None], from_next, from_second[None]])
    other_y = send(kept, along_y)
    other_y, rows_next, rows_second = lax.optimization_barrier((other_y, rows_next, rows_second))
    pack = jnp.concatenate([block[None], rows_next, rows_second[None]])
    full_rows = [pack, send(pack, along_yl)]
    full_rows += [send(part, across) for part in full_rows]
    mine = [kept, other_y, send(kept, pass_on), send(other_y, pass_on)]
    others = [send(pack, across) for pack in mine]

    scaled, sums = call(
        product,
        (f32(rows, cols), f32(groups, 8, rows)),
        [place("yh", "z", "core", "yl"), *full_rows, accum, col_scale[None], *mine, *others],
        flops=6 * rows * cols * depth * groups,
    )
    sums = lax.all_to_all(sums, COL, 0, 0)
    return call(divide, f32(rows, cols), [scaled, sums], scalars=0)


def solution(mesh):
    fine = Mesh(mesh.devices.reshape(SIZES), ALL)
    placed = (P(ROW, COL), P(ROW, COL), P(COL))
    return jax.shard_map(
        per_device, mesh=fine, in_specs=placed, out_specs=P(ROW, COL), check_vma=False
    )
```

```python
import itertools

import jax
import jax.numpy as jnp
from jax import lax
from jax.experimental import pallas as pl
from jax.experimental.pallas import tpu as pltpu
from jax.sharding import Mesh, PartitionSpec as P

YH, Z, CORE, YL, X = SIZES = 2, 8, 2, 2, 4
ROW = ("yh", "z", "core")
COL = ("yl", "x")
ALL = (*ROW, *COL)
VMEM = pl.BlockSpec(memory_space=pltpu.VMEM)
SMEM = pl.BlockSpec(memory_space=pltpu.SMEM)


def send(value, target):
    def index(place):
        found = 0
        for at, size in zip(place, SIZES, strict=True):
            found = found * size + at
        return found

    pairs = [(index(place), index(target(*place))) for place in itertools.product(*map(range, SIZES))]
    return lax.ppermute(value, ALL, pairs)


def across(yh, z, core, yl, x):
    return yh, z, 1 - core, yl, x


def along_z(hops):
    def target(yh, z, core, yl, x):
        return yl, (z + hops) % Z, core, yh, x

    return target


def pass_on(yh, z, core, yl, x):
    return yh, (z + (1 if core == 0 else -1)) % Z, core, yl, x


def along_x(hops):
    def target(yh, z, core, yl, x):
        return yh, z, core, yl, (x + hops) % X

    return target


def along_y(yh, z, core, yl, x):
    return 1 - yh, z, core, yl, x


def diagonal(yh, z, core, yl, x):
    return 1 - yh, (z + (1 if core == 0 else -1)) % Z, core, yl, x


def along_yl(yh, z, core, yl, x):
    return yh, z, core, 1 - yl, x


def sort_planes(place_ref, *refs):
    held, outs, sorted_ref = refs[:X], refs[X : 2 * X], refs[2 * X]
    z, x = (place_ref[i] for i in range(2))
    for step, piece in enumerate(held):
        sorted_ref[lax.rem(z // 2 - step - x + 2 * X, X)] = piece[...]
    for step, out in enumerate(outs):
        out[...] = sorted_ref[step]


def split(value):
    high = value.astype(jnp.bfloat16)
    low = (value - high.astype(jnp.float32)).astype(jnp.bfloat16)
    return high, low


def times(a, b):
    return lax.dot_general(a, b, (((0,), (0,)), ((), ())), preferred_element_type=jnp.float32)


def product(place_ref, rows0_ref, rows1_ref, rows2_ref, rows3_ref, accum_ref, scale_ref, *refs):
    packs, (scaled_ref, sums_ref) = (refs[:4], refs[4:8]), refs[8:]
    yh, z, core, yl = (place_ref[i] for i in range(4))
    at = lax.rem(yh + yl, 2)
    held = (rows0_ref, rows1_ref, rows2_ref, rows3_ref)
    high, low = split(jnp.concatenate([ref[at] for ref in held] + [ref[1 - at] for ref in held], axis=0))
    depth = high.shape[0]
    rows, width = rows0_ref.shape[2], refs[0].shape[2]
    squares = jnp.zeros((rows, 128), jnp.float32)
    for odd in range(2):
        for beside in range(CORE):
            pair = [packs[beside][2 * odd + i][...] for i in range(2)]
            block = jnp.concatenate(pair, axis=0).reshape(depth, width)
            block_high, block_low = split(block)
            part = times(high, block_high) + (times(high, block_low) + times(low, block_high))
            tile = lax.rem(z + odd, 2) * CORE + lax.rem(core + beside, CORE)
            cols = pl.ds(pl.multiple_of(tile * width, width), width)
            scaled = (accum_ref[:, cols] + part) * scale_ref[:, cols]
            scaled_ref[:, cols] = scaled
            for lane in range(0, width, 128):
                chunk = scaled[:, lane : lane + 128]
                squares += chunk * chunk
    sums = jnp.sum(squares.T, axis=0, keepdims=True)
    sums_ref[...] = jnp.broadcast_to(sums[None], sums_ref.shape)


def divide(scaled_ref, sums_ref, out_ref):
    rows, cols = scaled_ref.shape
    total = jnp.sum(sums_ref[...], axis=0)[:1]
    count = cols * sums_ref.shape[0]
    factor = lax.rsqrt(total / count + 1e-06)
    factor = jnp.broadcast_to(factor, (128, rows)).T
    for lane in range(0, cols, 128):
        out_ref[:, lane : lane + 128] = scaled_ref[:, lane : lane + 128] * factor


def call(kernel, out_shape, inputs, scalars=1, scratch=(), flops=0):
    return pl.pallas_call(
        kernel,
        out_shape=out_shape,
        in_specs=[SMEM] * scalars + [VMEM] * (len(inputs) - scalars),
        out_specs=jax.tree.map(lambda _: VMEM, out_shape),
        scratch_shapes=list(scratch),
        compiler_params=pltpu.CompilerParams(vmem_limit_bytes=16 * 1024 * 1024),
        cost_estimate=pl.CostEstimate(flops=flops, bytes_accessed=2 * 1024 * 1024, transcendentals=0),
    )(*inputs)


def f32(*shape):
    return jax.ShapeDtypeStruct(shape, jnp.float32)


def place(*names):
    return jnp.stack([lax.axis_index(name) for name in names])


def per_device(left_panel, accum, col_scale):
    block = left_panel.T
    depth, rows = block.shape
    cols = accum.shape[1]
    groups = YL * X

    held = [send(block, along_z(2 * step)) for step in range(X)]
    beside_yl = send(block, along_yl)
    planes = call(
        sort_planes,
        (f32(depth, rows),) * X,
        [place("z", "x"), *held],
        scratch=[pltpu.VMEM((X, depth, rows), jnp.float32)],
    )
    got = [send(planes[step], along_x(step)) for step in range(1, X)]
    kept = jnp.stack([planes[0], *got])
    _, beside_yl = lax.optimization_barrier((planes[1], beside_yl))
    pair = jnp.stack([block, beside_yl])
    from_x = [send(pair, along_x(step)) for step in range(1, X)]
    other_y = send(kept, along_y)
    passed = send(kept, pass_on)
    both_passed = send(kept, diagonal)
    other_y, *from_x = lax.optimization_barrier((other_y, *from_x))
    full_rows = [pair, *from_x]
    mine = [kept, other_y, passed, both_passed]
    others = [send(pack, across) for pack in mine]

    scaled, sums = call(
        product,
        (f32(rows, cols), f32(groups, 8, rows)),
        [place("yh", "z", "core", "yl"), *full_rows, accum, col_scale[None], *mine, *others],
        flops=6 * rows * cols * depth * groups,
    )
    sums = lax.all_to_all(sums, COL, 0, 0)
    return call(divide, f32(rows, cols), [scaled, sums], scalars=0)


def solution(mesh):
    fine = Mesh(mesh.devices.reshape(SIZES), ALL)
    placed = (P(ROW, COL), P(ROW, COL), P(COL))
    return jax.shard_map(
        per_device, mesh=fine, in_specs=placed, out_specs=P(ROW, COL), check_vma=False
    )
```

```python
import itertools

import jax
import jax.numpy as jnp
from jax import lax
from jax.experimental import pallas as pl
from jax.experimental.pallas import tpu as pltpu
from jax.sharding import Mesh, PartitionSpec as P

YH, Z, CORE, YL, X = SIZES = 2, 8, 2, 2, 4
ROW = ("yh", "z", "core")
COL = ("yl", "x")
ALL = (*ROW, *COL)
VMEM = pl.BlockSpec(memory_space=pltpu.VMEM)
SMEM = pl.BlockSpec(memory_space=pltpu.SMEM)


def send(value, target):
    def index(place):
        found = 0
        for at, size in zip(place, SIZES, strict=True):
            found = found * size + at
        return found

    pairs = [(index(place), index(target(*place))) for place in itertools.product(*map(range, SIZES))]
    return lax.ppermute(value, ALL, pairs)


def across(yh, z, core, yl, x):
    return yh, z, 1 - core, yl, x


def along_z(hops):
    def target(yh, z, core, yl, x):
        return yl, (z + hops) % Z, core, yh, x

    return target


def pass_on(yh, z, core, yl, x):
    return yh, (z + (1 if core == 0 else -1)) % Z, core, yl, x


def along_x(hops):
    def target(yh, z, core, yl, x):
        return yh, z, core, yl, (x + hops) % X

    return target


def along_y(yh, z, core, yl, x):
    return 1 - yh, z, core, yl, x


def diagonal(yh, z, core, yl, x):
    return 1 - yh, (z + (1 if core == 0 else -1)) % Z, core, yl, x


def along_yl(yh, z, core, yl, x):
    return yh, z, core, 1 - yl, x


def sort_planes(place_ref, *refs):
    held, outs, sorted_ref = refs[:X], refs[X : 2 * X], refs[2 * X]
    z, x = (place_ref[i] for i in range(2))
    for step, piece in enumerate(held):
        sorted_ref[lax.rem(z // 2 - step - x + 2 * X, X)] = piece[...]
    for step, out in enumerate(outs):
        out[...] = sorted_ref[step]


def split(value):
    high = value.astype(jnp.bfloat16)
    low = (value - high.astype(jnp.float32)).astype(jnp.bfloat16)
    return high, low


def times(a, b):
    return jnp.dot(a, b, preferred_element_type=jnp.float32)


def order_rows(place_ref, *refs):
    held, (high_ref, low_ref) = refs[:X], refs[X:]
    at = lax.rem(place_ref[0] + place_ref[1], 2)
    high, low = split(jnp.concatenate([ref[at] for ref in held] + [ref[1 - at] for ref in held], axis=0).T)
    high_ref[...] = high
    low_ref[...] = low


def product(place_ref, high_ref, low_ref, accum_ref, scale_ref, *refs):
    packs, (scaled_ref, sums_ref) = (refs[:4], refs[4:8]), refs[8:]
    z, core = place_ref[0], place_ref[1]
    high, low = high_ref[...], low_ref[...]
    rows, depth = high.shape
    width = refs[0].shape[2]
    squares = jnp.zeros((rows, 128), jnp.float32)
    for odd in range(2):
        for beside in range(CORE):
            pair = [packs[beside][2 * odd + i][...] for i in range(2)]
            block = jnp.concatenate(pair, axis=0).reshape(depth, width)
            block_high, block_low = split(block)
            part = times(high, block_high) + (times(high, block_low) + times(low, block_high))
            tile = lax.rem(z + odd, 2) * CORE + lax.rem(core + beside, CORE)
            cols = pl.ds(pl.multiple_of(tile * width, width), width)
            scaled = (accum_ref[:, cols] + part) * scale_ref[:, cols]
            scaled_ref[:, cols] = scaled
            for lane in range(0, width, 128):
                chunk = scaled[:, lane : lane + 128]
                squares += chunk * chunk
    sums = jnp.sum(squares.T, axis=0, keepdims=True)
    sums_ref[...] = jnp.broadcast_to(sums[None], sums_ref.shape)


def divide(scaled_ref, sums_ref, out_ref):
    rows, cols = scaled_ref.shape
    total = jnp.sum(sums_ref[...], axis=0)[:1]
    count = cols * sums_ref.shape[0]
    factor = lax.rsqrt(total / count + 1e-06)
    factor = jnp.broadcast_to(factor, (128, rows)).T
    for lane in range(0, cols, 128):
        out_ref[:, lane : lane + 128] = scaled_ref[:, lane : lane + 128] * factor


def call(kernel, out_shape, inputs, scalars=1, scratch=(), flops=0):
    return pl.pallas_call(
        kernel,
        out_shape=out_shape,
        in_specs=[SMEM] * scalars + [VMEM] * (len(inputs) - scalars),
        out_specs=jax.tree.map(lambda _: VMEM, out_shape),
        scratch_shapes=list(scratch),
        compiler_params=pltpu.CompilerParams(vmem_limit_bytes=16 * 1024 * 1024),
        cost_estimate=pl.CostEstimate(flops=flops, bytes_accessed=2 * 1024 * 1024, transcendentals=0),
    )(*inputs)


def f32(*shape):
    return jax.ShapeDtypeStruct(shape, jnp.float32)


def place(*names):
    return jnp.stack([lax.axis_index(name) for name in names])


def per_device(left_panel, accum, col_scale):
    block = left_panel.T
    depth, rows = block.shape
    cols = accum.shape[1]
    groups = YL * X

    held = [send(block, along_z(2 * step)) for step in range(X)]
    source, held[3] = lax.optimization_barrier((block, held[3]))
    beside_yl = send(source, along_yl)
    planes = call(
        sort_planes,
        (f32(depth, rows),) * X,
        [place("z", "x"), *held],
        scratch=[pltpu.VMEM((X, depth, rows), jnp.float32)],
    )
    got = [send(planes[step], along_x(step)) for step in range(1, X)]
    kept = jnp.stack([planes[0], *got])
    _, beside_yl = lax.optimization_barrier((planes[1], beside_yl))
    pair = jnp.stack([block, beside_yl])
    from_x = [send(pair, along_x(step)) for step in range(1, X)]
    other_y = send(kept, along_y)
    passed = send(kept, pass_on)
    both_passed = send(kept, diagonal)
    low_type = jax.ShapeDtypeStruct((rows, groups * depth), jnp.bfloat16)
    high, low = call(order_rows, (low_type, low_type), [place("yh", "yl"), pair, *from_x], flops=0)
    other_y, high = lax.optimization_barrier((other_y, high))
    mine = [kept, other_y, passed, both_passed]
    others = [send(pack, across) for pack in mine]

    scaled, sums = call(
        product,
        (f32(rows, cols), f32(groups, 8, rows)),
        [place("z", "core"), high, low, accum, col_scale[None], *mine, *others],
        flops=6 * rows * cols * depth * groups,
    )
    sums = lax.all_to_all(sums, COL, 0, 0)
    return call(divide, f32(rows, cols), [scaled, sums], scalars=0)


def solution(mesh):
    fine = Mesh(mesh.devices.reshape(SIZES), ALL)
    placed = (P(ROW, COL), P(ROW, COL), P(COL))
    return jax.shard_map(
        per_device, mesh=fine, in_specs=placed, out_specs=P(ROW, COL), check_vma=False
    )
```

```python
import itertools

import jax
import jax.numpy as jnp
from jax import lax
from jax.experimental import pallas as pl
from jax.experimental.pallas import tpu as pltpu
from jax.sharding import Mesh, PartitionSpec as P

YH, Z, CORE, YL, X = SIZES = 2, 8, 2, 2, 4
ROW = ("yh", "z", "core")
COL = ("yl", "x")
ALL = (*ROW, *COL)
VMEM = pl.BlockSpec(memory_space=pltpu.VMEM)
SMEM = pl.BlockSpec(memory_space=pltpu.SMEM)


def send(value, target):
    def index(place):
        found = 0
        for at, size in zip(place, SIZES, strict=True):
            found = found * size + at
        return found

    pairs = [(index(place), index(target(*place))) for place in itertools.product(*map(range, SIZES))]
    return lax.ppermute(value, ALL, pairs)


def across(yh, z, core, yl, x):
    return yh, z, 1 - core, yl, x


def along_z(hops):
    def target(yh, z, core, yl, x):
        return yl, (z + hops) % Z, core, yh, x

    return target


def pass_on(yh, z, core, yl, x):
    return yh, (z + (1 if core == 0 else -1)) % Z, core, yl, x


def along_x(hops):
    def target(yh, z, core, yl, x):
        return yh, z, core, yl, (x + hops) % X

    return target


def along_y(yh, z, core, yl, x):
    return 1 - yh, z, core, yl, x


def diagonal(yh, z, core, yl, x):
    return 1 - yh, (z + (1 if core == 0 else -1)) % Z, core, yl, x


def along_yl(yh, z, core, yl, x):
    return yh, z, core, 1 - yl, x


def sort_planes(place_ref, *refs):
    held, outs, sorted_ref = refs[:X], refs[X : 2 * X], refs[2 * X]
    z, x = (place_ref[i] for i in range(2))
    for step, piece in enumerate(held):
        sorted_ref[lax.rem(z // 2 - step - x + 2 * X, X)] = piece[...]
    for step, out in enumerate(outs):
        out[...] = sorted_ref[step]


def split(value):
    high = value.astype(jnp.bfloat16)
    low = (value - high.astype(jnp.float32)).astype(jnp.bfloat16)
    return high, low


def times(a, b):
    return jnp.dot(a, b, preferred_element_type=jnp.float32)


def order_rows(place_ref, *refs):
    held, (high_ref, low_ref) = refs[:X], refs[X:]
    at = lax.rem(place_ref[0] + place_ref[1], 2)
    high, low = split(jnp.concatenate([ref[at] for ref in held] + [ref[1 - at] for ref in held], axis=0).T)
    high_ref[...] = high
    low_ref[...] = low


def product(place_ref, high_ref, low_ref, accum_ref, scale_ref, *refs):
    packs, (scaled_ref, sums_ref) = (refs[:4], refs[4:8]), refs[8:]
    z, core = place_ref[0], place_ref[1]
    high, low = high_ref[...], low_ref[...]
    rows, depth = high.shape
    width = refs[0].shape[2]
    squares = jnp.zeros((rows, 128), jnp.float32)
    for odd in range(2):
        for beside in range(CORE):
            pair = [packs[beside][2 * odd + i][...] for i in range(2)]
            block = jnp.concatenate(pair, axis=0).reshape(depth, width)
            block_high, block_low = split(block)
            part = times(high, block_high) + (times(high, block_low) + times(low, block_high))
            tile = lax.rem(z + odd, 2) * CORE + lax.rem(core + beside, CORE)
            cols = pl.ds(pl.multiple_of(tile * width, width), width)
            scaled = (accum_ref[:, cols] + part) * scale_ref[:, cols]
            scaled_ref[:, cols] = scaled
            for lane in range(0, width, 128):
                chunk = scaled[:, lane : lane + 128]
                squares += chunk * chunk
    sums = jnp.sum(squares.T, axis=0, keepdims=True)
    sums_ref[...] = jnp.broadcast_to(sums[None], sums_ref.shape)


def divide(scaled_ref, sums_ref, out_ref):
    rows, cols = scaled_ref.shape
    total = jnp.sum(sums_ref[...], axis=0)[:1]
    count = cols * sums_ref.shape[0]
    factor = lax.rsqrt(total / count + 1e-06)
    factor = jnp.broadcast_to(factor, (128, rows)).T
    for lane in range(0, cols, 128):
        out_ref[:, lane : lane + 128] = scaled_ref[:, lane : lane + 128] * factor


def call(kernel, out_shape, inputs, scalars=1, scratch=(), flops=0):
    return pl.pallas_call(
        kernel,
        out_shape=out_shape,
        in_specs=[SMEM] * scalars + [VMEM] * (len(inputs) - scalars),
        out_specs=jax.tree.map(lambda _: VMEM, out_shape),
        scratch_shapes=list(scratch),
        compiler_params=pltpu.CompilerParams(vmem_limit_bytes=16 * 1024 * 1024),
        cost_estimate=pl.CostEstimate(flops=flops, bytes_accessed=2 * 1024 * 1024, transcendentals=0),
    )(*inputs)


def f32(*shape):
    return jax.ShapeDtypeStruct(shape, jnp.float32)


def place(*names):
    return jnp.stack([lax.axis_index(name) for name in names])


def per_device(left_panel, accum, col_scale):
    block = left_panel.T
    depth, rows = block.shape
    cols = accum.shape[1]
    groups = YL * X

    held = [send(block, along_z(2 * step)) for step in range(X)]
    source, held[3] = lax.optimization_barrier((block, held[3]))
    beside_yl = send(source, along_yl)
    planes = call(
        sort_planes,
        (f32(depth, rows),) * X,
        [place("z", "x"), *held],
        scratch=[pltpu.VMEM((X, depth, rows), jnp.float32)],
    )
    got = [send(planes[step], along_x(step)) for step in range(1, X)]
    kept = jnp.stack([planes[0], *got])
    _, beside_yl = lax.optimization_barrier((planes[1], beside_yl))
    pair = jnp.stack([block, beside_yl])
    from_x = [send(pair, along_x(step)) for step in range(1, X)]
    other_y = send(kept, along_y)
    passed = send(kept, pass_on)
    both_passed = send(kept, diagonal)
    low_type = jax.ShapeDtypeStruct((rows, groups * depth), jnp.bfloat16)
    high, low = call(order_rows, (low_type, low_type), [place("yh", "yl"), pair, *from_x], flops=0)
    both_passed, high = lax.optimization_barrier((both_passed, high))
    mine = [kept, other_y, passed, both_passed]
    others = [send(pack, across) for pack in mine]

    scaled, sums = call(
        product,
        (f32(rows, cols), f32(groups, 8, rows)),
        [place("z", "core"), high, low, accum, col_scale[None], *mine, *others],
        flops=6 * rows * cols * depth * groups,
    )
    sums = lax.all_to_all(sums, COL, 0, 0)
    return call(divide, f32(rows, cols), [scaled, sums], scalars=0)


def solution(mesh):
    fine = Mesh(mesh.devices.reshape(SIZES), ALL)
    placed = (P(ROW, COL), P(ROW, COL), P(COL))
    return jax.shard_map(
        per_device, mesh=fine, in_specs=placed, out_specs=P(ROW, COL), check_vma=False
    )
```
